32 devices in a mesh: wide: 16 (over z, y, x), narrow: 2 (over core).
Axes of the slice: x: 2, y: 2, z: 4, core: 2. Of those that a mesh axis runs over, the one named last changes fastest.
Arguments:
- source: float32 [16, 256, 256], P('narrow', 'wide'), may hold values from -8 to 8
- start_pressure: float32 [16, 256, 256], P('narrow', 'wide'), may hold values from -4 to 4
- reaction: float32 [16, 256, 256], P('narrow', 'wide'), may hold values from 0.003 to 0.03
- couplings: float32 [6, 16, 256, 256], P(None, 'narrow', 'wide'), may hold values from 0.3 to 3
- run_lengths: int32 [2, 4], replicated, may hold values from 1 to 8, 16 in all within a row
Outputs:
- pressure: float32 [16, 256, 256], P('narrow', 'wide')
- coarse_correction: float32 [8, 128, 128], P('narrow', 'wide')
The draws below stay inside these ranges and needn't reach their ends.
Inputs may be any that keep to these rules, and one draw needn't show every extreme that they name: `run_lengths`: each row lists, in order along the second dimension, the lengths of the runs of tile columns of that slab; a row sums to 16 and its largest entry is exactly 8.
All inputs are finite; a program needn't handle non-finite values.
Results may differ from the reference program's by a relative error of at most 0.00002.
Values sent between devices are 32-bit elements; how exact they have to be, the bound alone decides.
A program may use at most 64 MiB of HBM per device.

```python
import math
import jax
import jax.numpy as jnp
import numpy as np
from jax import lax

CZ = 8
CX = 16
NY = 256
SWEEPS = 4
COARSE_SWEEPS = 4
RUNS = 4
RUN_MOST = 8
NZ = 16
NX = 256
N_WIDE = 16
N_NARROW = 2


def shard_levels(stream_key, dims, shards, low, largest):
    gain = 1.0
    for dim, shards_of in shards:
        draws = jax.random.uniform(jax.random.fold_in(jax.random.fold_in(stream_key, 6), dim), (shards_of,), jnp.float32, low / len(shards), largest / len(shards))
        gain = gain * jnp.repeat(jnp.exp(draws), dims[dim] // shards_of).reshape((-1,) + (1,) * (len(dims) - 1 - dim))
    return gain


def split_up(count, total, bound, skew):
    loads = [(1 << 20) // math.isqrt(standing ** skew) + 1 for standing in range(2, count + 1)]
    surplus, counts = total - bound - (count - 1), [1] * (count - 1)
    while surplus > 0:
        movable = [i for i in range(count - 1) if counts[i] < bound]
        whole, remaining = sum([loads[i] for i in movable]), surplus
        for i in movable:
            addition = min(bound - counts[i], max(1, remaining * loads[i] // whole), surplus)
            counts[i] = counts[i] + addition
            surplus = surplus - addition
    return np.array([bound] + counts)


def ragged(stream_key, count, total, most, slope):
    if count == 2:
        one = jax.random.randint(stream_key, (), max(1, total - most), min(most, total - 1) + 1)
        return jnp.stack([one, total - one])
    lengths = jnp.asarray(split_up(count, total, most, slope), jnp.int32)
    twos = (count - 1) // 2
    donor, receiver = lengths[1:1 + 2 * twos:2], lengths[2:2 + 2 * twos:2]
    room = jnp.minimum(donor - 1, most - receiver)
    shifted = jax.random.randint(jax.random.fold_in(stream_key, 1), (twos,), 0, 1 << 20) % (room + 1)
    lengths = lengths.at[1:1 + 2 * twos:2].set(donor - shifted).at[2:2 + 2 * twos:2].set(receiver + shifted)
    return lengths[jax.random.permutation(jax.random.fold_in(stream_key, 2), count)]


def centred(stream_key, extent, scale, reach, shards=(), held_as=jnp.bfloat16):
    level = shard_levels(stream_key, extent, shards, -0.22, 0.18) if shards else 1.0
    array = jax.random.normal(stream_key, extent, jnp.float32) * scale * level
    return jnp.minimum(jnp.maximum(array, -reach), reach).astype(held_as)


def setup_inputs(seed: int = 0) -> dict:
    keys = jax.random.split(jax.random.key(seed), 6)
    source = centred(keys[0], (NZ, NX, NY), 2.0, 8.0, ((0, 2), (1, 16)), jnp.float32)
    start_pressure = centred(keys[1], (NZ, NX, NY), 0.5, 4.0, ((0, 2), (1, 16)), jnp.float32)
    reaction = jnp.clip(jnp.exp(math.log(0.03) - 2.3025851 * jax.random.uniform(keys[2], (NZ, NX, NY), jnp.float32) ** shard_levels(keys[2], (NZ, NX, NY), ((0, 2), (1, 16)), -0.2, 0.2)), 0.003, 0.03)
    couplings = jnp.clip(jnp.exp(math.log(3.0) - 2.3025851 * jax.random.uniform(keys[3], (6, NZ, NX, NY), jnp.float32) ** shard_levels(keys[3], (6, NZ, NX, NY), ((1, 2), (2, 16)), -0.2, 0.2)), 0.3, 3.0)
    run_lengths = jax.vmap(lambda own: ragged(own, RUNS, N_WIDE, RUN_MOST, 2))(jax.random.split(keys[4], N_NARROW)).reshape((N_NARROW, RUNS)).astype(jnp.int32)
    return dict(source=source, start_pressure=start_pressure, reaction=reaction, couplings=couplings, run_lengths=run_lengths)


def coupled(weights, padded):
    total = weights[0] * padded[:-2, 1:-1, 1:-1]
    total = total + weights[1] * padded[2:, 1:-1, 1:-1]
    total = total + weights[2] * padded[1:-1, :-2, 1:-1]
    total = total + weights[3] * padded[1:-1, 2:, 1:-1]
    total = total + weights[4] * padded[1:-1, 1:-1, :-2]
    total = total + weights[5] * padded[1:-1, 1:-1, 2:]
    return total


def checker(first_ids, second_ids, third_ids):
    return (first_ids[:, None, None] + second_ids[None, :, None] + third_ids[None, None, :]) % 2


def pad_axis(values, axis):
    widths = [(0, 0)] * values.ndim
    widths[axis] = (1, 1)
    return jnp.pad(values, widths)


def restrict_padded(padded, axis):
    length = padded.shape[axis] - 2

    def take(offset):
        return lax.slice_in_dim(padded, offset, offset + length - 1, 2, axis)

    return 0.25 * take(0) + 0.75 * take(1) + 0.75 * take(2) + 0.25 * take(3)


def face_sum(field, axis_pos, parity_bit):
    first, second, third = field.shape
    blocks = field.reshape(first // 2, 2, second // 2, 2, third // 2, 2)
    picked = lax.slice_in_dim(blocks, parity_bit, parity_bit + 1, 1, axis_pos)
    return jnp.sum(picked, axis=(1, 3, 5))


def coarse_fields(reaction, couplings):
    first, second, third = reaction.shape
    coarse_reaction = jnp.sum(reaction.reshape(first // 2, 2, second // 2, 2, third // 2, 2), axis=(1, 3, 5))
    faces = [face_sum(couplings[0], 1, 0), face_sum(couplings[1], 1, 1), face_sum(couplings[2], 3, 0),
             face_sum(couplings[3], 3, 1), face_sum(couplings[4], 5, 0), face_sum(couplings[5], 5, 1)]
    coarse_diag = coarse_reaction
    for channel in range(6):
        coarse_diag = coarse_diag + faces[channel]
    return coarse_diag, faces


def smooth(rhs_field, diagonal, weights, parity, start, sweeps):
    field = start
    for sweep_index in range(sweeps):
        for colour in range(2):
            updated = (rhs_field + coupled(weights, jnp.pad(field, 1))) / diagonal
            field = jnp.where(parity == colour, updated, field)
    return field


def prolong(coarse):
    first, second, third = coarse.shape
    wide_form = jnp.broadcast_to(coarse[:, None, :, None, :, None], (first, 2, second, 2, third, 2))
    return wide_form.reshape(2 * first, 2 * second, 2 * third)


def reference(source, start_pressure, reaction, couplings, run_lengths):
    diagonal = reaction
    for channel in range(6):
        diagonal = diagonal + couplings[channel]
    parity = checker(jnp.arange(NZ, dtype=jnp.int32), jnp.arange(NX, dtype=jnp.int32), jnp.arange(NY, dtype=jnp.int32))
    smoothed = smooth(source, diagonal, couplings, parity, start_pressure, SWEEPS)
    residual = source - (diagonal * smoothed - coupled(couplings, jnp.pad(smoothed, 1)))
    along_y = restrict_padded(pad_axis(residual, 2), 2)
    along_x = restrict_padded(pad_axis(along_y, 1), 1)
    coarse_rhs = restrict_padded(pad_axis(along_x, 0), 0)
    coarse_diag, faces = coarse_fields(reaction, couplings)
    half_depth = CZ // 2
    half_across = CX // 2
    coarse_z = jnp.arange(NZ // 2, dtype=jnp.int32)
    coarse_x = jnp.arange(NX // 2, dtype=jnp.int32)
    coarse_y = jnp.arange(NY // 2, dtype=jnp.int32)
    local_z = coarse_z % half_depth
    local_x = coarse_x % half_across
    slab_index = coarse_z // half_depth
    tile_index = coarse_x // half_across
    run_ends = jnp.cumsum(run_lengths, axis=1).astype(jnp.int32)
    run_begins = run_ends - run_lengths
    columns = jnp.arange(N_WIDE, dtype=jnp.int32)
    start_table = jnp.any(run_begins[:, :, None] == columns[None, None, :], axis=1)
    end_table = jnp.any(run_ends[:, :, None] - 1 == columns[None, None, :], axis=1)
    starts_here = start_table[slab_index[:, None], tile_index[None, :]]
    ends_here = end_table[slab_index[:, None], tile_index[None, :]]
    keep_down = (local_z != 0)[:, None, None]
    keep_up = (local_z != half_depth - 1)[:, None, None]
    keep_west = jnp.logical_not((local_x == 0)[None, :] & starts_here)[:, :, None]
    keep_east = jnp.logical_not((local_x == half_across - 1)[None, :] & ends_here)[:, :, None]
    kept = jnp.stack([jnp.where(keep_down, faces[0], 0.0), jnp.where(keep_up, faces[1], 0.0),
                      jnp.where(keep_west, faces[2], 0.0), jnp.where(keep_east, faces[3], 0.0),
                      faces[4], faces[5]])
    coarse_parity = checker(coarse_z, coarse_x, coarse_y)
    coarse_correction = smooth(coarse_rhs, coarse_diag, kept, coarse_parity,
                               jnp.zeros_like(coarse_rhs), COARSE_SWEEPS)
    pressure = smoothed + prolong(coarse_correction)
    return pressure, coarse_correction
```

```python
import functools

import jax
import jax.numpy as jnp
from jax import lax
from jax.experimental import pallas as pl
from jax.experimental.pallas import tpu as pltpu
from jax.sharding import PartitionSpec as P

SWEEPS = 4
COARSE_SWEEPS = 4
STEPS = 2 * SWEEPS
MESH = pl.DeviceIdType.MESH
DOT = functools.partial(
    jnp.dot, precision=lax.Precision.HIGHEST, preferred_element_type=jnp.float32
)


def iota(shape, dim):
    return lax.broadcasted_iota(jnp.int32, shape, dim)


def kernel(
    n_wide,
    n_narrow,
    lengths_ref,
    source_ref,
    start_ref,
    reaction_ref,
    couplings_ref,
    pressure_ref,
    correction_ref,
    field,
    weights,
    scaled,
    diag,
    x_low,
    x_high,
    z_low,
    z_high,
    x_stage,
    z_stage,
    sums,
    operator,
    window,
    edge_low,
    edge_high,
    edge_stage,
    own_stage,
    spread,
    send_sem,
    recv_sem,
    op_send,
    op_recv,
    rhs_send,
    rhs_recv,
):
    depth, across, height = source_ref.shape
    cz, cx, cy = depth // 2, across // 2, height // 2
    wide = lax.axis_index("wide")
    narrow = lax.axis_index("narrow")
    there = {-1: wide > 0, 0: None, 1: wide < n_wide - 1}
    above = {-1: narrow > 0, 0: None, 1: narrow < n_narrow - 1}

    def exists(dx, dz):
        if dx == 0:
            return above[dz]
        if dz == 0:
            return there[dx]
        return jnp.logical_and(there[dx], above[dz])

    def target(dx, dz):
        return {"wide": wide + dx, "narrow": narrow + dz}

    around = [(dx, dz) for dx in (-1, 0, 1) for dz in (-1, 0, 1) if (dx, dz) != (0, 0)]

    for ref in (x_low, x_high, z_low, z_high, operator, window, edge_low, edge_high):
        ref[...] = jnp.zeros(ref.shape, ref.dtype)

    barrier = pltpu.get_barrier_semaphore()
    for dx, dz in around:

        @pl.when(exists(dx, dz))
        def _(dx=dx, dz=dz):
            pl.semaphore_signal(
                barrier, inc=1, device_id=target(dx, dz), device_id_type=MESH
            )

    beside = jnp.where(wide > 0, 1, 0) + jnp.where(wide < n_wide - 1, 1, 0)
    over = jnp.where(narrow > 0, 1, 0) + jnp.where(narrow < n_narrow - 1, 1, 0)
    pl.semaphore_wait(barrier, (beside + 1) * (over + 1) - 1)

    def faces(step):
        sides = [
            (-1, 0, x_stage.at[step, 0], x_high.at[step], 0),
            (1, 0, x_stage.at[step, 1], x_low.at[step], 1),
            (0, -1, z_stage.at[step, 0], z_high.at[step], 2),
            (0, 1, z_stage.at[step, 1], z_low.at[step], 3),
        ]
        return [
            (
                exists(dx, dz),
                pltpu.make_async_remote_copy(
                    src_ref=src,
                    dst_ref=dst,
                    send_sem=send_sem.at[step, which],
                    recv_sem=recv_sem.at[step, which],
                    device_id=target(dx, dz),
                    device_id_type=MESH,
                ),
            )
            for dx, dz, src, dst, which in sides
        ]

    def arrivals(step):
        order = [(1, 0, 0), (-1, 0, 1), (0, 1, 2), (0, -1, 3)]
        copies = faces(step)
        return [(exists(dx, dz), copies[which][1]) for dx, dz, which in order]

    def send(step, values):
        x_stage[step, 0] = values[:, 0:1, :]
        x_stage[step, 1] = values[:, across - 1 : across, :]
        z_stage[step, 0] = values[0]
        z_stage[step, 1] = values[depth - 1]
        for here, copy in faces(step):
            pl.when(here)(copy.start)

    send(0, start_ref[...])
    field[...] = start_ref[...]

    total = reaction_ref[...]
    for channel in range(6):
        total = total + couplings_ref[channel]
    diag[...] = total
    inverse = 1.0 / total
    scaled[...] = source_ref[...] * inverse
    lane = iota((depth, across, height), 2)
    for channel in range(6):
        scaled_weight = couplings_ref[channel] * inverse
        if channel == 4:
            scaled_weight = jnp.where(lane == 0, 0.0, scaled_weight)
        if channel == 5:
            scaled_weight = jnp.where(lane == height - 1, 0.0, scaled_weight)
        weights[channel] = scaled_weight

    fine_y = iota((height, cy), 0)
    coarse_y = iota((height, cy), 1)
    even = jnp.where(fine_y == 2 * coarse_y, 1.0, 0.0)
    odd = jnp.where(fine_y == 2 * coarse_y + 1, 1.0, 0.0)

    def in_z(take):
        low, high = [], []
        for z in range(cz):
            low.append(take(2 * z))
            high.append(take(2 * z + 1))
        return jnp.stack(low), jnp.stack(high)

    parts = []
    low, high = in_z(lambda z: reaction_ref[z])
    parts.append(low + high)
    parts.append(in_z(lambda z: couplings_ref[0, z])[0])
    parts.append(in_z(lambda z: couplings_ref[1, z])[1])
    for channel in (2, 3, 4, 5):
        low, high = in_z(lambda z: couplings_ref[channel, z])
        parts.append(low + high)
    for place, part in enumerate(parts):
        flat = part.reshape(cz * across, height)
        matrix = even if place == 5 else odd if place == 6 else even + odd
        sums[place] = DOT(flat, matrix).reshape(cz, across, cy)

    def pick(place, which):
        return sums[place, :, pl.ds(which, cx, stride=2), :]

    coarse = [pick(place, 0) + pick(place, 1) for place in (0, 1, 2)]
    coarse += [pick(3, 0), pick(4, 1)]
    coarse += [pick(place, 0) + pick(place, 1) for place in (5, 6)]
    coarse_diag = coarse[0]
    for channel in range(6):
        coarse_diag = coarse_diag + coarse[1 + channel]
    begin = jnp.int32(0)
    starts = jnp.int32(0)
    ends = jnp.int32(0)
    for run in range(lengths_ref.shape[1]):
        end = begin + lengths_ref[narrow, run]
        starts = starts + jnp.where(begin == wide, 1, 0)
        ends = ends + jnp.where(end - 1 == wide, 1, 0)
        begin = end
    block = (cz, cx, cy)
    at_z, at_x, at_y = iota(block, 0), iota(block, 1), iota(block, 2)
    cuts = [
        at_z == 0,
        at_z == cz - 1,
        jnp.where(at_x == 0, starts, 0) > 0,
        jnp.where(at_x == cx - 1, ends, 0) > 0,
        at_y == 0,
        at_y == cy - 1,
    ]
    coarse_inverse = 1.0 / coarse_diag
    for channel in range(6):
        operator[channel, :, cx : 2 * cx, :] = jnp.where(
            cuts[channel], 0.0, coarse[1 + channel] * coarse_inverse
        )
    operator[6, :, cx : 2 * cx, :] = coarse_inverse

    def operator_copy(dx, which):
        start = cx - cx * dx
        return pltpu.make_async_remote_copy(
            src_ref=operator.at[:, :, cx : 2 * cx, :],
            dst_ref=operator.at[:, :, start : start + cx, :],
            send_sem=op_send.at[which],
            recv_sem=op_recv.at[which],
            device_id=target(dx, 0),
            device_id_type=MESH,
        )

    for which, dx in enumerate((-1, 1)):
        pl.when(exists(dx, 0))(operator_copy(dx, which).start)

    row = iota((depth, across, height), 1)
    parity = (iota((depth, across, height), 0) + row + lane) % 2

    def relaxed(step):
        for here, copy in arrivals(step):
            pl.when(here)(copy.wait_recv)
        v = field[...]
        out = scaled[...]
        out = out + weights[0] * jnp.concatenate([z_low[step][None], v[:-1]], axis=0)
        out = out + weights[1] * jnp.concatenate([v[1:], z_high[step][None]], axis=0)
        west = jnp.where(row == 0, x_low[step], pltpu.roll(v, 1, 1))
        out = out + weights[2] * west
        east = jnp.where(row == across - 1, x_high[step], pltpu.roll(v, across - 1, 1))
        out = out + weights[3] * east
        out = out + weights[4] * pltpu.roll(v, 1, 2)
        out = out + weights[5] * pltpu.roll(v, height - 1, 2)
        return v, out

    def half_sweep(step, carry):
        v, out = relaxed(step)
        v = jnp.where(parity == step % 2, out, v)
        field[...] = v
        send(step + 1, v)
        return carry

    lax.fori_loop(0, STEPS, half_sweep, 0)
    v, out = relaxed(STEPS)
    residual = diag[...] * (out - v)

    offset = fine_y - 2 * coarse_y
    restrict = jnp.where(
        (offset == 0) | (offset == 1), 0.75, jnp.where((offset == -1) | (offset == 2), 0.25, 0.0)
    )
    along_y = DOT(residual.reshape(depth * across, height), restrict)
    along_y = along_y.reshape(depth, across, cy)
    edge_stage[0] = 0.25 * along_y[0]
    edge_stage[1] = 0.25 * along_y[depth - 1]
    base = 8
    own = base + across
    for z in range(cz):
        value = 0.75 * along_y[2 * z] + 0.75 * along_y[2 * z + 1]
        if z > 0:
            value = value + 0.25 * along_y[2 * z - 1]
        if z < cz - 1:
            value = value + 0.25 * along_y[2 * z + 2]
        window[z, own : own + across, :] = value
        own_stage[z] = value

    def window_copy(dx, dz, which):
        start = own - across * dx
        rows = slice(start, start + across)
        if dz == 0:
            src, dst = own_stage, window.at[:, rows, :]
        elif dz < 0:
            src, dst = edge_stage.at[0], edge_high.at[rows, :]
        else:
            src, dst = edge_stage.at[1], edge_low.at[rows, :]
        return pltpu.make_async_remote_copy(
            src_ref=src,
            dst_ref=dst,
            send_sem=rhs_send.at[which],
            recv_sem=rhs_recv.at[which],
            device_id=target(dx, dz),
            device_id_type=MESH,
        )

    for which, (dx, dz) in enumerate(around):
        pl.when(exists(dx, dz))(window_copy(dx, dz, which).start)
    for which, (dx, dz) in enumerate(around):
        pl.when(exists(-dx, -dz))(window_copy(dx, dz, which).wait_recv)
    for which, dx in enumerate((-1, 1)):
        pl.when(exists(-dx, 0))(operator_copy(dx, which).wait_recv)

    window[0] = window[0] + edge_low[...]
    window[cz - 1] = window[cz - 1] + edge_high[...]
    span = 3 * cx

    def take(offset):
        return window[:, pl.ds(base + offset, span, stride=2), :]

    rhs = 0.25 * take(-1) + 0.75 * take(0) + 0.75 * take(1) + 0.25 * take(2)
    rhs = rhs * operator[6]
    shape = (cz, span, cy)
    coarse_parity = (iota(shape, 0) + iota(shape, 1) + cx + iota(shape, 2)) % 2
    result = jnp.where(coarse_parity == 0, rhs, 0.0)
    for half in range(1, 2 * COARSE_SWEEPS):
        u = result
        out = rhs
        out = out + operator[0] * jnp.concatenate([u[-1:], u[:-1]], axis=0)
        out = out + operator[1] * jnp.concatenate([u[1:], u[:1]], axis=0)
        out = out + operator[2] * pltpu.roll(u, 1, 1)
        out = out + operator[3] * pltpu.roll(u, span - 1, 1)
        out = out + operator[4] * pltpu.roll(u, 1, 2)
        out = out + operator[5] * pltpu.roll(u, cy - 1, 2)
        result = jnp.where(coarse_parity == half % 2, out, u)

    correction = result[:, cx : 2 * cx, :]
    correction_ref[...] = correction
    flat = correction.reshape(cz * cx, cy)
    repeat = jnp.where(iota((cy, height), 0) == iota((cy, height), 1) // 2, 1.0, 0.0)
    wider = DOT(flat, repeat).reshape(cz, cx, height)
    for half in range(height // cy):
        piece = wider[:, :, half * cy : (half + 1) * cy]
        for which in range(2):
            spread[half, :, pl.ds(which, cx, stride=2), :] = piece
    for z in range(depth):
        for half in range(height // cy):
            lanes = slice(half * cy, (half + 1) * cy)
            pressure_ref[z, :, lanes] = field[z, :, lanes] + spread[half, z // 2]

    def drain(step, carry):
        for here, copy in faces(step):
            pl.when(here)(copy.wait_send)
        return carry

    lax.fori_loop(0, STEPS + 1, drain, 0)
    for which, dx in enumerate((-1, 1)):
        pl.when(exists(dx, 0))(operator_copy(dx, which).wait_send)
    for which, (dx, dz) in enumerate(around):
        pl.when(exists(dx, dz))(window_copy(dx, dz, which).wait_send)


def body(n_wide, n_narrow, source, start_pressure, reaction, couplings, run_lengths):
    depth, across, height = source.shape
    cz, cx, cy = depth // 2, across // 2, height // 2
    f32 = jnp.float32
    fine = (depth, across, height)
    rounds = STEPS + 1
    vmem = pl.BlockSpec(memory_space=pltpu.VMEM)
    return pl.pallas_call(
        functools.partial(kernel, n_wide, n_narrow),
        out_shape=(
            jax.ShapeDtypeStruct(fine, f32),
            jax.ShapeDtypeStruct((cz, cx, cy), f32),
        ),
        in_specs=[pl.BlockSpec(memory_space=pltpu.SMEM)] + [vmem] * 4,
        out_specs=(vmem, vmem),
        scratch_shapes=[
            pltpu.VMEM(fine, f32),
            pltpu.VMEM((6,) + fine, f32),
            pltpu.VMEM(fine, f32),
            pltpu.VMEM(fine, f32),
            pltpu.VMEM((rounds, depth, 1, height), f32),
            pltpu.VMEM((rounds, depth, 1, height), f32),
            pltpu.VMEM((rounds, across, height), f32),
            pltpu.VMEM((rounds, across, height), f32),
            pltpu.VMEM((rounds, 2, depth, 1, height), f32),
            pltpu.VMEM((rounds, 2, across, height), f32),
            pltpu.VMEM((7, cz, across, cy), f32),
            pltpu.VMEM((7, cz, 3 * cx, cy), f32),
            pltpu.VMEM((cz, 3 * across + 16, cy), f32),
            pltpu.VMEM((3 * across + 16, cy), f32),
            pltpu.VMEM((3 * across + 16, cy), f32),
            pltpu.VMEM((2, across, cy), f32),
            pltpu.VMEM((cz, across, cy), f32),
            pltpu.VMEM((2, cz, across, cy), f32),
            pltpu.SemaphoreType.DMA((rounds, 4)),
            pltpu.SemaphoreType.DMA((rounds, 4)),
            pltpu.SemaphoreType.DMA((2,)),
            pltpu.SemaphoreType.DMA((2,)),
            pltpu.SemaphoreType.DMA((8,)),
            pltpu.SemaphoreType.DMA((8,)),
        ],
        compiler_params=pltpu.CompilerParams(
            collective_id=0, has_side_effects=True, vmem_limit_bytes=32 * 1024 * 1024
        ),
    )(run_lengths, source, start_pressure, reaction, couplings)


def solution(mesh):
    placed = (
        P("narrow", "wide", None),
        P("narrow", "wide", None),
        P("narrow", "wide", None),
        P(None, "narrow", "wide", None),
        P(),
    )
    return jax.shard_map(
        functools.partial(body, mesh.shape["wide"], mesh.shape["narrow"]),
        mesh=mesh,
        in_specs=placed,
        out_specs=(P("narrow", "wide", None), P("narrow", "wide", None)),
        check_vma=False,
    )
```

```python
import functools

import jax
import jax.numpy as jnp
from jax import lax
from jax.experimental import pallas as pl
from jax.experimental.pallas import tpu as pltpu
from jax.sharding import PartitionSpec as P

SWEEPS = 4
COARSE_SWEEPS = 4
STEPS = 2 * SWEEPS
DEEP = 3
ROUNDS = (STEPS + DEEP) // DEEP
MESH = pl.DeviceIdType.MESH
DOT = functools.partial(
    jnp.dot, precision=lax.Precision.HIGHEST, preferred_element_type=jnp.float32
)


def iota(shape, dim):
    return lax.broadcasted_iota(jnp.int32, shape, dim)


def kernel(
    n_wide,
    n_narrow,
    lengths_ref,
    source_hbm,
    start_hbm,
    reaction_hbm,
    couplings_hbm,
    pressure_ref,
    correction_ref,
    source_ref,
    reaction_ref,
    couplings_ref,
    field,
    weights,
    diag,
    halo,
    x_stage,
    border,
    halo_weights,
    weight_stage,
    z_low,
    z_high,
    z_stage,
    sums,
    operator,
    window,
    edge_low,
    edge_high,
    edge_stage,
    own_stage,
    spread,
    load_sem,
    x_send,
    x_recv,
    z_send,
    z_recv,
    w_send,
    w_recv,
    op_send,
    op_recv,
    rhs_send,
    rhs_recv,
):
    depth, across, height = field.shape
    cz, cx, cy = depth // 2, across // 2, height // 2
    wide = lax.axis_index("wide")
    narrow = lax.axis_index("narrow")
    there = {-1: wide > 0, 0: None, 1: wide < n_wide - 1}
    above = {-1: narrow > 0, 0: None, 1: narrow < n_narrow - 1}

    def exists(dx, dz):
        if dx == 0:
            return above[dz]
        if dz == 0:
            return there[dx]
        return jnp.logical_and(there[dx], above[dz])

    def target(dx, dz):
        return {"wide": wide + dx, "narrow": narrow + dz}

    around = [(dx, dz) for dx in (-1, 0, 1) for dz in (-1, 0, 1) if (dx, dz) != (0, 0)]

    loads = [
        pltpu.make_async_copy(src, dst, load_sem.at[which])
        for which, (src, dst) in enumerate(
            (
                (start_hbm, field),
                (reaction_hbm, reaction_ref),
                (couplings_hbm, couplings_ref),
                (source_hbm, source_ref),
            )
        )
    ]
    for load in loads:
        load.start()

    for ref in (halo, halo_weights, z_low, z_high, operator, window, edge_low, edge_high):
        ref[...] = jnp.zeros(ref.shape, ref.dtype)

    barrier = pltpu.get_barrier_semaphore()
    for dx, dz in around:

        @pl.when(exists(dx, dz))
        def _(dx=dx, dz=dz):
            pl.semaphore_signal(
                barrier, inc=1, device_id=target(dx, dz), device_id_type=MESH
            )

    def remote(src, dst, send, recv, dx, dz):
        return pltpu.make_async_remote_copy(
            src_ref=src,
            dst_ref=dst,
            send_sem=send,
            recv_sem=recv,
            device_id=target(dx, dz),
            device_id_type=MESH,
        )

    def x_copy(turn, side):
        return remote(
            x_stage.at[turn, side], halo.at[turn, 1 - side],
            x_send.at[turn, side], x_recv.at[turn, side], 2 * side - 1, 0,
        )

    def weight_copy(side):
        return remote(
            weight_stage.at[side], halo_weights.at[1 - side],
            w_send.at[side], w_recv.at[side], 2 * side - 1, 0,
        )

    def z_copy(step, side):
        return remote(
            z_stage.at[step, side], (z_low if side else z_high).at[step],
            z_send.at[step, side], z_recv.at[step, side], 0, 2 * side - 1,
        )

    def start_x(copy):
        for side in range(2):
            pl.when(there[2 * side - 1])(copy(side).start)

    def arrive_x(copy):
        for side in range(2):
            pl.when(there[1 - 2 * side])(copy(side).wait_recv)

    def pack(store, layers):
        for side in range(2):
            for layer in range(layers):
                at = across - 1 - layer if side else layer
                for z in range(depth):
                    store(side, layer, z, at)

    def send_x(turn):
        def store(side, layer, z, at):
            x_stage[turn, side, layer, z : z + 1, :] = field[z, at : at + 1, :]

        pack(store, DEEP)
        start_x(functools.partial(x_copy, turn))

    for load in loads:
        load.wait()
    total = reaction_ref[...]
    for channel in range(6):
        total = total + couplings_ref[channel]
    diag[...] = total
    inverse = 1.0 / total
    lane = iota((depth, across, height), 2)
    for channel in range(6):
        scaled_weight = couplings_ref[channel] * inverse
        if channel == 4:
            scaled_weight = jnp.where(lane == 0, 0.0, scaled_weight)
        if channel == 5:
            scaled_weight = jnp.where(lane == height - 1, 0.0, scaled_weight)
        weights[channel] = scaled_weight
    weights[6] = source_ref[...] * inverse

    def store_weights(side, layer, z, at):
        for place in range(7):
            weight_stage[side, layer, place, z : z + 1, :] = weights[place, z, at : at + 1, :]

    pack(store_weights, DEEP - 1)

    beside = jnp.where(wide > 0, 1, 0) + jnp.where(wide < n_wide - 1, 1, 0)
    over = jnp.where(narrow > 0, 1, 0) + jnp.where(narrow < n_narrow - 1, 1, 0)
    pl.semaphore_wait(barrier, (beside + 1) * (over + 1) - 1)
    send_x(0)
    start_x(weight_copy)

    fine_y = iota((height, cy), 0)
    coarse_y = iota((height, cy), 1)
    even = jnp.where(fine_y == 2 * coarse_y, 1.0, 0.0)
    odd = jnp.where(fine_y == 2 * coarse_y + 1, 1.0, 0.0)

    def in_z(take):
        low, high = [], []
        for z in range(cz):
            low.append(take(2 * z))
            high.append(take(2 * z + 1))
        return jnp.stack(low), jnp.stack(high)

    parts = []
    low, high = in_z(lambda z: reaction_ref[z])
    parts.append(low + high)
    parts.append(in_z(lambda z: couplings_ref[0, z])[0])
    parts.append(in_z(lambda z: couplings_ref[1, z])[1])
    for channel in (2, 3, 4, 5):
        low, high = in_z(lambda z: couplings_ref[channel, z])
        parts.append(low + high)
    for place, part in enumerate(parts):
        flat = part.reshape(cz * across, height)
        matrix = even if place == 5 else odd if place == 6 else even + odd
        sums[place] = DOT(flat, matrix).reshape(cz, across, cy)

    def pick(place, which):
        return sums[place, :, pl.ds(which, cx, stride=2), :]

    coarse = [pick(place, 0) + pick(place, 1) for place in (0, 1, 2)]
    coarse += [pick(3, 0), pick(4, 1)]
    coarse += [pick(place, 0) + pick(place, 1) for place in (5, 6)]
    coarse_diag = coarse[0]
    for channel in range(6):
        coarse_diag = coarse_diag + coarse[1 + channel]
    begin = jnp.int32(0)
    starts = jnp.int32(0)
    ends = jnp.int32(0)
    for run in range(lengths_ref.shape[1]):
        end = begin + lengths_ref[narrow, run]
        starts = starts + jnp.where(begin == wide, 1, 0)
        ends = ends + jnp.where(end - 1 == wide, 1, 0)
        begin = end
    block = (cz, cx, cy)
    at_z, at_x, at_y = iota(block, 0), iota(block, 1), iota(block, 2)
    cuts = [
        at_z == 0,
        at_z == cz - 1,
        jnp.where(at_x == 0, starts, 0) > 0,
        jnp.where(at_x == cx - 1, ends, 0) > 0,
        at_y == 0,
        at_y == cy - 1,
    ]
    coarse_inverse = 1.0 / coarse_diag
    for channel in range(6):
        operator[channel, :, cx : 2 * cx, :] = jnp.where(
            cuts[channel], 0.0, coarse[1 + channel] * coarse_inverse
        )
    operator[6, :, cx : 2 * cx, :] = coarse_inverse

    def operator_copy(side):
        start = 0 if side else 2 * cx
        return remote(
            operator.at[:, :, cx : 2 * cx, :], operator.at[:, :, start : start + cx, :],
            op_send.at[side], op_recv.at[side], 2 * side - 1, 0,
        )

    row = iota((across, height), 0)
    tile = row + iota((across, height), 1)
    layer_row = iota((depth, height), 0)
    layer_tile = layer_row + iota((depth, height), 1)
    top = depth - 1

    def exchange_z(step, turn):
        for side, z in enumerate((0, top)):
            z_stage[step, side, :across, :] = field[z]
            for beside in range(2):
                for layer in range(DEEP - 1):
                    at = across + beside * (DEEP - 1) + layer
                    z_stage[step, side, at : at + 1, :] = halo[turn, beside, layer, z : z + 1, :]
        for side in range(2):
            pl.when(above[2 * side - 1])(z_copy(step, side).start)
        for side in range(2):
            pl.when(above[1 - 2 * side])(z_copy(step, side).wait_recv)

    def relaxed(z, step, sides):
        v = field[z]
        below = field[z - 1] if z > 0 else z_low[step, :across, :]
        over = field[z + 1] if z < top else z_high[step, :across, :]
        out = weights[6, z] + weights[0, z] * below + weights[1, z] * over
        west = jnp.where(row == 0, sides[0][z : z + 1, :], pltpu.roll(v, 1, 0))
        out = out + weights[2, z] * west
        east = jnp.where(row == across - 1, sides[1][z : z + 1, :], pltpu.roll(v, across - 1, 0))
        out = out + weights[3, z] * east
        out = out + weights[4, z] * pltpu.roll(v, 1, 1)
        out = out + weights[5, z] * pltpu.roll(v, height - 1, 1)
        return v, out

    def relax_layer(step, turn, side, layer, inner, outer):
        h = halo[turn, side, layer]
        w = halo_weights.at[side, layer]
        at = across + side * (DEEP - 1) + layer
        below = jnp.where(layer_row == 0, z_low[step, at : at + 1, :], pltpu.roll(h, 1, 0))
        over = jnp.where(layer_row == top, z_high[step, at : at + 1, :], pltpu.roll(h, top, 0))
        west, east = (inner, outer) if side else (outer, inner)
        out = w[6] + w[0] * below + w[1] * over + w[2] * west + w[3] * east
        out = out + w[4] * pltpu.roll(h, 1, 1) + w[5] * pltpu.roll(h, height - 1, 1)
        colour = layer_tile + step + (layer if side else layer + 1)
        halo[turn, side, layer] = jnp.where(colour % 2 == 0, out, h)

    def pack_border(side, layer, z, at):
        border[side, z : z + 1, :] = field[z, at : at + 1, :]

    def half_sweep(turn, inside):
        step = turn * DEEP + inside
        exchange_z(step, turn)
        colours = [(tile + step + z) % 2 == 0 for z in range(2)]
        for z in range(depth):
            v, out = relaxed(z, step, [halo.at[turn, side, 0] for side in range(2)])
            field[z] = jnp.where(colours[z % 2], out, v)
        if inside == 0:

            @pl.when(turn == 0)
            def _():
                arrive_x(weight_copy)

        for layer in range(DEEP - 1 - inside):
            for side in range(2):
                inner = border[side] if layer == 0 else halo[turn, side, layer - 1]
                relax_layer(step, turn, side, layer, inner, halo[turn, side, layer + 1])
        if inside < DEEP - 1:
            pack(pack_border, 1)

    def exchange_x(turn):
        @pl.when(turn > 0)
        def _():
            send_x(turn)

        @pl.when(turn == 1)
        def _():
            start_x(operator_copy)

        pack(pack_border, 1)
        arrive_x(functools.partial(x_copy, turn))

    def full_round(turn, carry):
        exchange_x(turn)
        for inside in range(DEEP):
            half_sweep(turn, inside)
        return carry

    last = ROUNDS - 1
    lax.fori_loop(0, last, full_round, 0)
    exchange_x(last)
    for inside in range(STEPS - last * DEEP):
        half_sweep(last, inside)
    exchange_z(STEPS, last)
    residual = []
    for z in range(depth):
        v, out = relaxed(z, STEPS, [halo.at[last, side, 0] for side in range(2)])
        residual.append(diag[z] * (out - v))
    residual = jnp.stack(residual)

    offset = fine_y - 2 * coarse_y
    restrict = jnp.where(
        (offset == 0) | (offset == 1), 0.75, jnp.where((offset == -1) | (offset == 2), 0.25, 0.0)
    )
    along_y = DOT(residual.reshape(depth * across, height), restrict)
    along_y = along_y.reshape(depth, across, cy)
    edge_stage[0] = 0.25 * along_y[0]
    edge_stage[1] = 0.25 * along_y[depth - 1]
    base = 8
    own = base + across
    for z in range(cz):
        value = 0.75 * along_y[2 * z] + 0.75 * along_y[2 * z + 1]
        if z > 0:
            value = value + 0.25 * along_y[2 * z - 1]
        if z < cz - 1:
            value = value + 0.25 * along_y[2 * z + 2]
        window[z, own : own + across, :] = value
        own_stage[z] = value

    def window_copy(dx, dz, which):
        start = own - across * dx
        rows = slice(start, start + across)
        if dz == 0:
            src, dst = own_stage, window.at[:, rows, :]
        elif dz < 0:
            src, dst = edge_stage.at[0], edge_high.at[rows, :]
        else:
            src, dst = edge_stage.at[1], edge_low.at[rows, :]
        return pltpu.make_async_remote_copy(
            src_ref=src,
            dst_ref=dst,
            send_sem=rhs_send.at[which],
            recv_sem=rhs_recv.at[which],
            device_id=target(dx, dz),
            device_id_type=MESH,
        )

    for which, (dx, dz) in enumerate(around):
        pl.when(exists(dx, dz))(window_copy(dx, dz, which).start)
    for which, (dx, dz) in enumerate(around):
        pl.when(exists(-dx, -dz))(window_copy(dx, dz, which).wait_recv)
    arrive_x(operator_copy)

    window[0] = window[0] + edge_low[...]
    window[cz - 1] = window[cz - 1] + edge_high[...]
    span = 3 * cx

    def take(offset):
        return window[:, pl.ds(base + offset, span, stride=2), :]

    rhs = 0.25 * take(-1) + 0.75 * take(0) + 0.75 * take(1) + 0.25 * take(2)
    rhs = rhs * operator[6]
    shape = (cz, span, cy)
    coarse_parity = (iota(shape, 0) + iota(shape, 1) + cx + iota(shape, 2)) % 2
    result = jnp.where(coarse_parity == 0, rhs, 0.0)
    for half in range(1, 2 * COARSE_SWEEPS):
        u = result
        out = rhs
        out = out + operator[0] * jnp.concatenate([u[-1:], u[:-1]], axis=0)
        out = out + operator[1] * jnp.concatenate([u[1:], u[:1]], axis=0)
        out = out + operator[2] * pltpu.roll(u, 1, 1)
        out = out + operator[3] * pltpu.roll(u, span - 1, 1)
        out = out + operator[4] * pltpu.roll(u, 1, 2)
        out = out + operator[5] * pltpu.roll(u, cy - 1, 2)
        result = jnp.where(coarse_parity == half % 2, out, u)

    correction = result[:, cx : 2 * cx, :]
    correction_ref[...] = correction
    flat = correction.reshape(cz * cx, cy)
    repeat = jnp.where(iota((cy, height), 0) == iota((cy, height), 1) // 2, 1.0, 0.0)
    wider = DOT(flat, repeat).reshape(cz, cx, height)
    for half in range(height // cy):
        piece = wider[:, :, half * cy : (half + 1) * cy]
        for which in range(2):
            spread[half, :, pl.ds(which, cx, stride=2), :] = piece
    for z in range(depth):
        for half in range(height // cy):
            lanes = slice(half * cy, (half + 1) * cy)
            pressure_ref[z, :, lanes] = field[z, :, lanes] + spread[half, z // 2]

    def drain_z(step, carry):
        for side in range(2):
            pl.when(above[2 * side - 1])(z_copy(step, side).wait_send)
        return carry

    def drain_x(copy):
        for side in range(2):
            pl.when(there[2 * side - 1])(copy(side).wait_send)

    lax.fori_loop(0, STEPS + 1, drain_z, 0)
    for turn in range(ROUNDS):
        drain_x(functools.partial(x_copy, turn))
    drain_x(weight_copy)
    drain_x(operator_copy)
    for which, (dx, dz) in enumerate(around):
        pl.when(exists(dx, dz))(window_copy(dx, dz, which).wait_send)


def body(n_wide, n_narrow, source, start_pressure, reaction, couplings, run_lengths):
    depth, across, height = source.shape
    cz, cx, cy = depth // 2, across // 2, height // 2
    f32 = jnp.float32
    fine = (depth, across, height)
    steps = STEPS + 1
    layers = DEEP - 1
    face = across + 2 * layers
    dma = pltpu.SemaphoreType.DMA
    hbm = pl.BlockSpec(memory_space=pltpu.HBM)
    vmem = pl.BlockSpec(memory_space=pltpu.VMEM)
    return pl.pallas_call(
        functools.partial(kernel, n_wide, n_narrow),
        out_shape=(
            jax.ShapeDtypeStruct(fine, f32),
            jax.ShapeDtypeStruct((cz, cx, cy), f32),
        ),
        in_specs=[pl.BlockSpec(memory_space=pltpu.SMEM)] + [hbm] * 4,
        out_specs=(vmem, vmem),
        scratch_shapes=[
            pltpu.VMEM(fine, f32),
            pltpu.VMEM(fine, f32),
            pltpu.VMEM((6,) + fine, f32),
            pltpu.VMEM(fine, f32),
            pltpu.VMEM((7,) + fine, f32),
            pltpu.VMEM(fine, f32),
            pltpu.VMEM((ROUNDS, 2, DEEP, depth, height), f32),
            pltpu.VMEM((ROUNDS, 2, DEEP, depth, height), f32),
            pltpu.VMEM((2, depth, height), f32),
            pltpu.VMEM((2, layers, 7, depth, height), f32),
            pltpu.VMEM((2, layers, 7, depth, height), f32),
            pltpu.VMEM((steps, face, height), f32),
            pltpu.VMEM((steps, face, height), f32),
            pltpu.VMEM((steps, 2, face, height), f32),
            pltpu.VMEM((7, cz, across, cy), f32),
            pltpu.VMEM((7, cz, 3 * cx, cy), f32),
            pltpu.VMEM((cz, 3 * across + 16, cy), f32),
            pltpu.VMEM((3 * across + 16, cy), f32),
            pltpu.VMEM((3 * across + 16, cy), f32),
            pltpu.VMEM((2, across, cy), f32),
            pltpu.VMEM((cz, across, cy), f32),
            pltpu.VMEM((2, cz, across, cy), f32),
            dma((4,)),
            dma((ROUNDS, 2)),
            dma((ROUNDS, 2)),
            dma((steps, 2)),
            dma((steps, 2)),
            dma((2,)),
            dma((2,)),
            dma((2,)),
            dma((2,)),
            dma((8,)),
            dma((8,)),
        ],
        compiler_params=pltpu.CompilerParams(
            collective_id=0, has_side_effects=True, vmem_limit_bytes=32 * 1024 * 1024
        ),
    )(run_lengths, source, start_pressure, reaction, couplings)


def solution(mesh):
    placed = (
        P("narrow", "wide", None),
        P("narrow", "wide", None),
        P("narrow", "wide", None),
        P(None, "narrow", "wide", None),
        P(),
    )
    return jax.shard_map(
        functools.partial(body, mesh.shape["wide"], mesh.shape["narrow"]),
        mesh=mesh,
        in_specs=placed,
        out_specs=(P("narrow", "wide", None), P("narrow", "wide", None)),
        check_vma=False,
    )
```

```python
import functools

import jax
import jax.numpy as jnp
from jax import lax
from jax.experimental import pallas as pl
from jax.experimental.pallas import tpu as pltpu
from jax.sharding import PartitionSpec as P

SWEEPS = 4
COARSE_SWEEPS = 4
STEPS = 2 * SWEEPS
DEEP = 3
ROUNDS = (STEPS + DEEP) // DEEP
MESH = pl.DeviceIdType.MESH
DOT = functools.partial(
    jnp.dot, precision=lax.Precision.HIGHEST, preferred_element_type=jnp.float32
)


def iota(shape, dim):
    return lax.broadcasted_iota(jnp.int32, shape, dim)


def kernel(
    n_wide,
    n_narrow,
    lengths_ref,
    source_hbm,
    start_hbm,
    reaction_hbm,
    couplings_hbm,
    pressure_ref,
    correction_ref,
    source_ref,
    reaction_ref,
    couplings_ref,
    field,
    weights,
    diag,
    halo,
    x_stage,
    border,
    halo_weights,
    weight_stage,
    z_low,
    z_high,
    z_stage,
    layer_low,
    layer_high,
    layer_stage,
    sums,
    operator,
    window,
    edge_low,
    edge_high,
    edge_stage,
    own_stage,
    spread,
    load_sem,
    x_send,
    x_recv,
    z_send,
    z_recv,
    layer_send,
    layer_recv,
    w_send,
    w_recv,
    op_send,
    op_recv,
    rhs_send,
    rhs_recv,
):
    depth, across, height = field.shape
    cz, cx, cy = depth // 2, across // 2, height // 2
    wide = lax.axis_index("wide")
    narrow = lax.axis_index("narrow")
    there = {-1: wide > 0, 0: None, 1: wide < n_wide - 1}
    above = {-1: narrow > 0, 0: None, 1: narrow < n_narrow - 1}

    def exists(dx, dz):
        if dx == 0:
            return above[dz]
        if dz == 0:
            return there[dx]
        return jnp.logical_and(there[dx], above[dz])

    def target(dx, dz):
        return {"wide": wide + dx, "narrow": narrow + dz}

    around = [(dx, dz) for dx in (-1, 0, 1) for dz in (-1, 0, 1) if (dx, dz) != (0, 0)]

    loads = [
        pltpu.make_async_copy(src, dst, load_sem.at[which])
        for which, (src, dst) in enumerate(
            (
                (start_hbm, field),
                (reaction_hbm, reaction_ref),
                (couplings_hbm, couplings_ref),
                (source_hbm, source_ref),
            )
        )
    ]
    for load in loads:
        load.start()

    for ref in (halo, halo_weights, z_low, z_high, layer_low, layer_high, operator, window, edge_low, edge_high):
        ref[...] = jnp.zeros(ref.shape, ref.dtype)

    barrier = pltpu.get_barrier_semaphore()
    for dx, dz in around:

        @pl.when(exists(dx, dz))
        def _(dx=dx, dz=dz):
            pl.semaphore_signal(
                barrier, inc=1, device_id=target(dx, dz), device_id_type=MESH
            )

    def remote(src, dst, send, recv, dx, dz):
        return pltpu.make_async_remote_copy(
            src_ref=src,
            dst_ref=dst,
            send_sem=send,
            recv_sem=recv,
            device_id=target(dx, dz),
            device_id_type=MESH,
        )

    def x_copy(turn, side):
        return remote(
            x_stage.at[turn, side], halo.at[turn, 1 - side],
            x_send.at[turn, side], x_recv.at[turn, side], 2 * side - 1, 0,
        )

    def weight_copy(side):
        return remote(
            weight_stage.at[side], halo_weights.at[1 - side],
            w_send.at[side], w_recv.at[side], 2 * side - 1, 0,
        )

    def z_copy(step, side):
        return remote(
            z_stage.at[step, side], (z_low if side else z_high).at[step],
            z_send.at[step, side], z_recv.at[step, side], 0, 2 * side - 1,
        )

    def layer_copy(step, side):
        return remote(
            layer_stage.at[step, side], (layer_low if side else layer_high).at[step],
            layer_send.at[step, side], layer_recv.at[step, side], 0, 2 * side - 1,
        )

    def start_z(copy):
        for side in range(2):
            pl.when(above[2 * side - 1])(copy(side).start)

    def arrive_z(copy):
        for side in range(2):
            pl.when(above[1 - 2 * side])(copy(side).wait_recv)

    def start_x(copy):
        for side in range(2):
            pl.when(there[2 * side - 1])(copy(side).start)

    def arrive_x(copy):
        for side in range(2):
            pl.when(there[1 - 2 * side])(copy(side).wait_recv)

    def pack(store, layers):
        for side in range(2):
            for layer in range(layers):
                at = across - 1 - layer if side else layer
                for z in range(depth):
                    store(side, layer, z, at)

    def send_x(turn):
        def store(side, layer, z, at):
            x_stage[turn, side, layer, z : z + 1, :] = field[z, at : at + 1, :]

        pack(store, DEEP)
        start_x(functools.partial(x_copy, turn))

    top = depth - 1

    def send_z(step):
        for side, z in enumerate((0, top)):
            z_stage[step, side] = field[z]
        start_z(functools.partial(z_copy, step))

    for load in loads:
        load.wait()
    total = reaction_ref[...]
    for channel in range(6):
        total = total + couplings_ref[channel]
    diag[...] = total
    inverse = 1.0 / total
    lane = iota((depth, across, height), 2)
    for channel in range(6):
        scaled_weight = couplings_ref[channel] * inverse
        if channel == 4:
            scaled_weight = jnp.where(lane == 0, 0.0, scaled_weight)
        if channel == 5:
            scaled_weight = jnp.where(lane == height - 1, 0.0, scaled_weight)
        weights[channel] = scaled_weight
    weights[6] = source_ref[...] * inverse

    def store_weights(side, layer, z, at):
        for place in range(7):
            weight_stage[side, layer, place, z : z + 1, :] = weights[place, z, at : at + 1, :]

    pack(store_weights, DEEP - 1)

    beside = jnp.where(wide > 0, 1, 0) + jnp.where(wide < n_wide - 1, 1, 0)
    over = jnp.where(narrow > 0, 1, 0) + jnp.where(narrow < n_narrow - 1, 1, 0)
    pl.semaphore_wait(barrier, (beside + 1) * (over + 1) - 1)
    send_x(0)
    start_x(weight_copy)
    send_z(0)

    fine_y = iota((height, cy), 0)
    coarse_y = iota((height, cy), 1)
    even = jnp.where(fine_y == 2 * coarse_y, 1.0, 0.0)
    odd = jnp.where(fine_y == 2 * coarse_y + 1, 1.0, 0.0)

    def in_z(take):
        low, high = [], []
        for z in range(cz):
            low.append(take(2 * z))
            high.append(take(2 * z + 1))
        return jnp.stack(low), jnp.stack(high)

    parts = []
    low, high = in_z(lambda z: reaction_ref[z])
    parts.append(low + high)
    parts.append(in_z(lambda z: couplings_ref[0, z])[0])
    parts.append(in_z(lambda z: couplings_ref[1, z])[1])
    for channel in (2, 3, 4, 5):
        low, high = in_z(lambda z: couplings_ref[channel, z])
        parts.append(low + high)
    for place, part in enumerate(parts):
        flat = part.reshape(cz * across, height)
        matrix = even if place == 5 else odd if place == 6 else even + odd
        sums[place] = DOT(flat, matrix).reshape(cz, across, cy)

    def pick(place, which):
        return sums[place, :, pl.ds(which, cx, stride=2), :]

    coarse = [pick(place, 0) + pick(place, 1) for place in (0, 1, 2)]
    coarse += [pick(3, 0), pick(4, 1)]
    coarse += [pick(place, 0) + pick(place, 1) for place in (5, 6)]
    coarse_diag = coarse[0]
    for channel in range(6):
        coarse_diag = coarse_diag + coarse[1 + channel]
    begin = jnp.int32(0)
    starts = jnp.int32(0)
    ends = jnp.int32(0)
    for run in range(lengths_ref.shape[1]):
        end = begin + lengths_ref[narrow, run]
        starts = starts + jnp.where(begin == wide, 1, 0)
        ends = ends + jnp.where(end - 1 == wide, 1, 0)
        begin = end
    block = (cz, cx, cy)
    at_z, at_x, at_y = iota(block, 0), iota(block, 1), iota(block, 2)
    cuts = [
        at_z == 0,
        at_z == cz - 1,
        jnp.where(at_x == 0, starts, 0) > 0,
        jnp.where(at_x == cx - 1, ends, 0) > 0,
        at_y == 0,
        at_y == cy - 1,
    ]
    coarse_inverse = 1.0 / coarse_diag
    for channel in range(6):
        operator[channel, :, cx : 2 * cx, :] = jnp.where(
            cuts[channel], 0.0, coarse[1 + channel] * coarse_inverse
        )
    operator[6, :, cx : 2 * cx, :] = coarse_inverse

    def operator_copy(channel, side):
        start = 0 if side else 2 * cx
        return remote(
            operator.at[channel, :, cx : 2 * cx, :],
            operator.at[channel, :, start : start + cx, :],
            op_send.at[channel, side], op_recv.at[channel, side], 2 * side - 1, 0,
        )

    row = iota((across, height), 0)
    tile = row + iota((across, height), 1)
    layer_row = iota((depth, height), 0)
    layer_tile = layer_row + iota((depth, height), 1)

    def send_layers(step, turn):
        for side, z in enumerate((0, top)):
            for beside in range(2):
                for layer in range(DEEP - 1):
                    at = beside * (DEEP - 1) + layer
                    layer_stage[step, side, at : at + 1, :] = halo[turn, beside, layer, z : z + 1, :]
        start_z(functools.partial(layer_copy, step))

    def relaxed(z, step, sides):
        v = field[z]
        below = field[z - 1] if z > 0 else z_low[step]
        over = field[z + 1] if z < top else z_high[step]
        out = weights[6, z] + weights[0, z] * below + weights[1, z] * over
        west = jnp.where(row == 0, sides[0][z : z + 1, :], pltpu.roll(v, 1, 0))
        out = out + weights[2, z] * west
        east = jnp.where(row == across - 1, sides[1][z : z + 1, :], pltpu.roll(v, across - 1, 0))
        out = out + weights[3, z] * east
        out = out + weights[4, z] * pltpu.roll(v, 1, 1)
        out = out + weights[5, z] * pltpu.roll(v, height - 1, 1)
        return v, out

    def relax_layer(step, turn, side, layer, inner, outer):
        h = halo[turn, side, layer]
        w = halo_weights.at[side, layer]
        at = side * (DEEP - 1) + layer
        below = jnp.where(layer_row == 0, layer_low[step, at : at + 1, :], pltpu.roll(h, 1, 0))
        over = jnp.where(layer_row == top, layer_high[step, at : at + 1, :], pltpu.roll(h, top, 0))
        west, east = (inner, outer) if side else (outer, inner)
        out = w[6] + w[0] * below + w[1] * over + w[2] * west + w[3] * east
        out = out + w[4] * pltpu.roll(h, 1, 1) + w[5] * pltpu.roll(h, height - 1, 1)
        colour = layer_tile + step + (layer if side else layer + 1)
        halo[turn, side, layer] = jnp.where(colour % 2 == 0, out, h)

    def pack_border(side, layer, z, at):
        border[side, z : z + 1, :] = field[z, at : at + 1, :]

    inner_planes = list(range(1, top))

    def half_sweep(turn, inside):
        step = turn * DEEP + inside
        colours = [(tile + step + z) % 2 == 0 for z in range(2)]

        def update(z):
            v, out = relaxed(z, step, [halo.at[turn, side, 0] for side in range(2)])
            field[z] = jnp.where(colours[z % 2], out, v)

        arrive_z(functools.partial(z_copy, step))
        update(0)
        update(top)
        send_z(step + 1)

        @pl.when(step > 0)
        def _():
            start_x(functools.partial(operator_copy, step - 1))

        for z in inner_planes:
            update(z)
        if inside < DEEP - 1:
            if inside == 0:

                @pl.when(turn == 0)
                def _():
                    arrive_x(weight_copy)

            arrive_z(functools.partial(layer_copy, step))
            for layer in range(DEEP - 1 - inside):
                for side in range(2):
                    if layer > 0:
                        inner = halo[turn, side, layer - 1]
                    else:
                        inner = border[side] if inside else x_stage[turn, side, 0]
                    relax_layer(step, turn, side, layer, inner, halo[turn, side, layer + 1])
            if inside + 1 < DEEP - 1:
                send_layers(step + 1, turn)
                pack(pack_border, 1)

    def exchange_x(turn):
        @pl.when(turn > 0)
        def _():
            send_x(turn)

        arrive_x(functools.partial(x_copy, turn))
        send_layers(turn * DEEP, turn)

    def full_round(turn, carry):
        exchange_x(turn)
        for inside in range(DEEP):
            half_sweep(turn, inside)
        return carry

    last = ROUNDS - 1
    lax.fori_loop(0, last, full_round, 0)
    exchange_x(last)
    for inside in range(STEPS - last * DEEP):
        half_sweep(last, inside)
    residual = [None] * depth

    def take_residual(z):
        v, out = relaxed(z, STEPS, [halo.at[last, side, 0] for side in range(2)])
        residual[z] = diag[z] * (out - v)

    for z in inner_planes:
        take_residual(z)
    arrive_z(functools.partial(z_copy, STEPS))
    take_residual(0)
    take_residual(top)
    residual = jnp.stack(residual)

    offset = fine_y - 2 * coarse_y
    restrict = jnp.where(
        (offset == 0) | (offset == 1), 0.75, jnp.where((offset == -1) | (offset == 2), 0.25, 0.0)
    )
    along_y = DOT(residual.reshape(depth * across, height), restrict)
    along_y = along_y.reshape(depth, across, cy)
    edge_stage[0] = 0.25 * along_y[0]
    edge_stage[1] = 0.25 * along_y[depth - 1]
    base = 8
    own = base + across
    for z in range(cz):
        value = 0.75 * along_y[2 * z] + 0.75 * along_y[2 * z + 1]
        if z > 0:
            value = value + 0.25 * along_y[2 * z - 1]
        if z < cz - 1:
            value = value + 0.25 * along_y[2 * z + 2]
        window[z, own : own + across, :] = value
        own_stage[z] = value

    def window_copy(dx, dz, which):
        start = own - across * dx
        rows = slice(start, start + across)
        if dz == 0:
            src, dst = own_stage, window.at[:, rows, :]
        elif dz < 0:
            src, dst = edge_stage.at[0], edge_high.at[rows, :]
        else:
            src, dst = edge_stage.at[1], edge_low.at[rows, :]
        return pltpu.make_async_remote_copy(
            src_ref=src,
            dst_ref=dst,
            send_sem=rhs_send.at[which],
            recv_sem=rhs_recv.at[which],
            device_id=target(dx, dz),
            device_id_type=MESH,
        )

    for which, (dx, dz) in enumerate(around):
        pl.when(exists(dx, dz))(window_copy(dx, dz, which).start)
    for which, (dx, dz) in enumerate(around):
        pl.when(exists(-dx, -dz))(window_copy(dx, dz, which).wait_recv)
    for channel in range(7):
        arrive_x(functools.partial(operator_copy, channel))

    window[0] = window[0] + edge_low[...]
    window[cz - 1] = window[cz - 1] + edge_high[...]
    span = 3 * cx

    def take(offset):
        return window[:, pl.ds(base + offset, span, stride=2), :]

    rhs = 0.25 * take(-1) + 0.75 * take(0) + 0.75 * take(1) + 0.25 * take(2)
    rhs = rhs * operator[6]
    shape = (cz, span, cy)
    coarse_parity = (iota(shape, 0) + iota(shape, 1) + cx + iota(shape, 2)) % 2
    result = jnp.where(coarse_parity == 0, rhs, 0.0)
    for half in range(1, 2 * COARSE_SWEEPS):
        u = result
        out = rhs
        out = out + operator[0] * jnp.concatenate([u[-1:], u[:-1]], axis=0)
        out = out + operator[1] * jnp.concatenate([u[1:], u[:1]], axis=0)
        out = out + operator[2] * pltpu.roll(u, 1, 1)
        out = out + operator[3] * pltpu.roll(u, span - 1, 1)
        out = out + operator[4] * pltpu.roll(u, 1, 2)
        out = out + operator[5] * pltpu.roll(u, cy - 1, 2)
        result = jnp.where(coarse_parity == half % 2, out, u)

    correction = result[:, cx : 2 * cx, :]
    correction_ref[...] = correction
    flat = correction.reshape(cz * cx, cy)
    repeat = jnp.where(iota((cy, height), 0) == iota((cy, height), 1) // 2, 1.0, 0.0)
    wider = DOT(flat, repeat).reshape(cz, cx, height)
    for half in range(height // cy):
        piece = wider[:, :, half * cy : (half + 1) * cy]
        for which in range(2):
            spread[half, :, pl.ds(which, cx, stride=2), :] = piece
    for z in range(depth):
        for half in range(height // cy):
            lanes = slice(half * cy, (half + 1) * cy)
            pressure_ref[z, :, lanes] = field[z, :, lanes] + spread[half, z // 2]

    def drain_z(copy):
        def one(step, carry):
            for side in range(2):
                pl.when(above[2 * side - 1])(copy(step, side).wait_send)
            return carry

        return one

    def drain_x(copy):
        for side in range(2):
            pl.when(there[2 * side - 1])(copy(side).wait_send)

    lax.fori_loop(0, STEPS + 1, drain_z(z_copy), 0)
    for step in range(STEPS):
        if step % DEEP < DEEP - 1:
            drain_z(layer_copy)(step, 0)
    for turn in range(ROUNDS):
        drain_x(functools.partial(x_copy, turn))
    drain_x(weight_copy)
    for channel in range(7):
        drain_x(functools.partial(operator_copy, channel))
    for which, (dx, dz) in enumerate(around):
        pl.when(exists(dx, dz))(window_copy(dx, dz, which).wait_send)


def body(n_wide, n_narrow, source, start_pressure, reaction, couplings, run_lengths):
    depth, across, height = source.shape
    cz, cx, cy = depth // 2, across // 2, height // 2
    f32 = jnp.float32
    fine = (depth, across, height)
    steps = STEPS + 1
    layers = DEEP - 1
    face = 2 * layers
    dma = pltpu.SemaphoreType.DMA
    hbm = pl.BlockSpec(memory_space=pltpu.HBM)
    vmem = pl.BlockSpec(memory_space=pltpu.VMEM)
    return pl.pallas_call(
        functools.partial(kernel, n_wide, n_narrow),
        out_shape=(
            jax.ShapeDtypeStruct(fine, f32),
            jax.ShapeDtypeStruct((cz, cx, cy), f32),
        ),
        in_specs=[pl.BlockSpec(memory_space=pltpu.SMEM)] + [hbm] * 4,
        out_specs=(vmem, vmem),
        scratch_shapes=[
            pltpu.VMEM(fine, f32),
            pltpu.VMEM(fine, f32),
            pltpu.VMEM((6,) + fine, f32),
            pltpu.VMEM(fine, f32),
            pltpu.VMEM((7,) + fine, f32),
            pltpu.VMEM(fine, f32),
            pltpu.VMEM((ROUNDS, 2, DEEP, depth, height), f32),
            pltpu.VMEM((ROUNDS, 2, DEEP, depth, height), f32),
            pltpu.VMEM((2, depth, height), f32),
            pltpu.VMEM((2, layers, 7, depth, height), f32),
            pltpu.VMEM((2, layers, 7, depth, height), f32),
            pltpu.VMEM((steps, across, height), f32),
            pltpu.VMEM((steps, across, height), f32),
            pltpu.VMEM((steps, 2, across, height), f32),
            pltpu.VMEM((steps, face, height), f32),
            pltpu.VMEM((steps, face, height), f32),
            pltpu.VMEM((steps, 2, face, height), f32),
            pltpu.VMEM((7, cz, across, cy), f32),
            pltpu.VMEM((7, cz, 3 * cx, cy), f32),
            pltpu.VMEM((cz, 3 * across + 16, cy), f32),
            pltpu.VMEM((3 * across + 16, cy), f32),
            pltpu.VMEM((3 * across + 16, cy), f32),
            pltpu.VMEM((2, across, cy), f32),
            pltpu.VMEM((cz, across, cy), f32),
            pltpu.VMEM((2, cz, across, cy), f32),
            dma((4,)),
            dma((ROUNDS, 2)),
            dma((ROUNDS, 2)),
            dma((steps, 2)),
            dma((steps, 2)),
            dma((steps, 2)),
            dma((steps, 2)),
            dma((2,)),
            dma((2,)),
            dma((7, 2)),
            dma((7, 2)),
            dma((8,)),
            dma((8,)),
        ],
        compiler_params=pltpu.CompilerParams(
            collective_id=0, has_side_effects=True, vmem_limit_bytes=32 * 1024 * 1024
        ),
    )(run_lengths, source, start_pressure, reaction, couplings)


def solution(mesh):
    placed = (
        P("narrow", "wide", None),
        P("narrow", "wide", None),
        P("narrow", "wide", None),
        P(None, "narrow", "wide", None),
        P(),
    )
    return jax.shard_map(
        functools.partial(body, mesh.shape["wide"], mesh.shape["narrow"]),
        mesh=mesh,
        in_specs=placed,
        out_specs=(P("narrow", "wide", None), P("narrow", "wide", None)),
        check_vma=False,
    )
```

```python
import functools

import jax
import jax.numpy as jnp
from jax import lax
from jax.experimental import pallas as pl
from jax.experimental.pallas import tpu as pltpu
from jax.sharding import PartitionSpec as P

SWEEPS = 4
COARSE_SWEEPS = 4
STEPS = 2 * SWEEPS
DEEP = 3
ROUNDS = (STEPS + DEEP) // DEEP
MESH = pl.DeviceIdType.MESH
DOT = functools.partial(
    jnp.dot, precision=lax.Precision.HIGHEST, preferred_element_type=jnp.float32
)


def iota(shape, dim):
    return lax.broadcasted_iota(jnp.int32, shape, dim)


def kernel(
    n_wide,
    n_narrow,
    lengths_ref,
    source_hbm,
    start_hbm,
    reaction_hbm,
    couplings_hbm,
    pressure_ref,
    correction_ref,
    source_ref,
    reaction_ref,
    couplings_ref,
    field,
    weights,
    diag,
    halo,
    x_stage,
    border,
    halo_weights,
    weight_stage,
    z_low,
    z_high,
    z_stage,
    layer_low,
    layer_high,
    layer_stage,
    sums,
    operator,
    window,
    edge_low,
    edge_high,
    edge_stage,
    own_stage,
    spread,
    load_sem,
    x_send,
    x_recv,
    z_send,
    z_recv,
    layer_send,
    layer_recv,
    w_send,
    w_recv,
    op_send,
    op_recv,
    rhs_send,
    rhs_recv,
):
    depth, across, height = field.shape
    cz, cx, cy = depth // 2, across // 2, height // 2
    wide = lax.axis_index("wide")
    narrow = lax.axis_index("narrow")
    there = {-1: wide > 0, 0: None, 1: wide < n_wide - 1}
    above = {-1: narrow > 0, 0: None, 1: narrow < n_narrow - 1}

    def exists(dx, dz):
        if dx == 0:
            return above[dz]
        if dz == 0:
            return there[dx]
        return jnp.logical_and(there[dx], above[dz])

    def target(dx, dz):
        return {"wide": wide + dx, "narrow": narrow + dz}

    around = [(dx, dz) for dx in (-1, 0, 1) for dz in (-1, 0, 1) if (dx, dz) != (0, 0)]

    loads = [
        pltpu.make_async_copy(src, dst, load_sem.at[which])
        for which, (src, dst) in enumerate(
            (
                (start_hbm, field),
                (reaction_hbm, reaction_ref),
                (couplings_hbm, couplings_ref),
                (source_hbm, source_ref),
            )
        )
    ]
    for load in loads:
        load.start()

    for ref in (halo, halo_weights, z_low, z_high, layer_low, layer_high, operator, window, edge_low, edge_high):
        ref[...] = jnp.zeros(ref.shape, ref.dtype)

    barrier = pltpu.get_barrier_semaphore()
    for dx, dz in around:

        @pl.when(exists(dx, dz))
        def _(dx=dx, dz=dz):
            pl.semaphore_signal(
                barrier, inc=1, device_id=target(dx, dz), device_id_type=MESH
            )

    def remote(src, dst, send, recv, dx, dz):
        return pltpu.make_async_remote_copy(
            src_ref=src,
            dst_ref=dst,
            send_sem=send,
            recv_sem=recv,
            device_id=target(dx, dz),
            device_id_type=MESH,
        )

    def x_copy(turn, side):
        return remote(
            x_stage.at[turn, side], halo.at[turn, 1 - side],
            x_send.at[turn, side], x_recv.at[turn, side], 2 * side - 1, 0,
        )

    def weight_copy(layer, side):
        return remote(
            weight_stage.at[side, layer], halo_weights.at[1 - side, layer],
            w_send.at[layer, side], w_recv.at[layer, side], 2 * side - 1, 0,
        )

    def z_copy(step, side):
        return remote(
            z_stage.at[step, side], (z_low if side else z_high).at[step],
            z_send.at[step, side], z_recv.at[step, side], 0, 2 * side - 1,
        )

    def layer_copy(step, side):
        return remote(
            layer_stage.at[step, side], (layer_low if side else layer_high).at[step],
            layer_send.at[step, side], layer_recv.at[step, side], 0, 2 * side - 1,
        )

    def start_z(copy):
        for side in range(2):
            pl.when(above[2 * side - 1])(copy(side).start)

    def arrive_z(copy):
        for side in range(2):
            pl.when(above[1 - 2 * side])(copy(side).wait_recv)

    def start_x(copy):
        for side in range(2):
            pl.when(there[2 * side - 1])(copy(side).start)

    def arrive_x(copy):
        for side in range(2):
            pl.when(there[1 - 2 * side])(copy(side).wait_recv)

    def pack(store, layers):
        for side in range(2):
            for layer in range(layers):
                at = across - 1 - layer if side else layer
                for z in range(depth):
                    store(side, layer, z, at)

    def send_x(turn):
        def store(side, layer, z, at):
            x_stage[turn, side, layer, z : z + 1, :] = field[z, at : at + 1, :]

        pack(store, DEEP)
        start_x(functools.partial(x_copy, turn))

    top = depth - 1

    def send_z(step):
        for side, z in enumerate((0, top)):
            z_stage[step, side] = field[z]
        start_z(functools.partial(z_copy, step))

    for load in loads:
        load.wait()
    total = reaction_ref[...]
    for channel in range(6):
        total = total + couplings_ref[channel]
    diag[...] = total
    inverse = 1.0 / total
    lane = iota((depth, across, height), 2)
    for channel in range(6):
        scaled_weight = couplings_ref[channel] * inverse
        if channel == 4:
            scaled_weight = jnp.where(lane == 0, 0.0, scaled_weight)
        if channel == 5:
            scaled_weight = jnp.where(lane == height - 1, 0.0, scaled_weight)
        weights[channel] = scaled_weight
    weights[6] = source_ref[...] * inverse

    def store_weights(side, layer, z, at):
        for place in range(7):
            weight_stage[side, layer, place, z : z + 1, :] = weights[place, z, at : at + 1, :]

    pack(store_weights, DEEP - 1)

    beside = jnp.where(wide > 0, 1, 0) + jnp.where(wide < n_wide - 1, 1, 0)
    over = jnp.where(narrow > 0, 1, 0) + jnp.where(narrow < n_narrow - 1, 1, 0)
    pl.semaphore_wait(barrier, (beside + 1) * (over + 1) - 1)
    send_x(0)
    for layer in range(DEEP - 1):
        start_x(functools.partial(weight_copy, layer))
    send_z(0)

    fine_y = iota((height, cy), 0)
    coarse_y = iota((height, cy), 1)
    even = jnp.where(fine_y == 2 * coarse_y, 1.0, 0.0)
    odd = jnp.where(fine_y == 2 * coarse_y + 1, 1.0, 0.0)

    def in_z(take):
        low, high = [], []
        for z in range(cz):
            low.append(take(2 * z))
            high.append(take(2 * z + 1))
        return jnp.stack(low), jnp.stack(high)

    parts = []
    low, high = in_z(lambda z: reaction_ref[z])
    parts.append(low + high)
    parts.append(in_z(lambda z: couplings_ref[0, z])[0])
    parts.append(in_z(lambda z: couplings_ref[1, z])[1])
    for channel in (2, 3, 4, 5):
        low, high = in_z(lambda z: couplings_ref[channel, z])
        parts.append(low + high)
    for place, part in enumerate(parts):
        flat = part.reshape(cz * across, height)
        matrix = even if place == 5 else odd if place == 6 else even + odd
        sums[place] = DOT(flat, matrix).reshape(cz, across, cy)

    def pick(place, which):
        return sums[place, :, pl.ds(which, cx, stride=2), :]

    coarse = [pick(place, 0) + pick(place, 1) for place in (0, 1, 2)]
    coarse += [pick(3, 0), pick(4, 1)]
    coarse += [pick(place, 0) + pick(place, 1) for place in (5, 6)]
    coarse_diag = coarse[0]
    for channel in range(6):
        coarse_diag = coarse_diag + coarse[1 + channel]
    begin = jnp.int32(0)
    starts = jnp.int32(0)
    ends = jnp.int32(0)
    for run in range(lengths_ref.shape[1]):
        end = begin + lengths_ref[narrow, run]
        starts = starts + jnp.where(begin == wide, 1, 0)
        ends = ends + jnp.where(end - 1 == wide, 1, 0)
        begin = end
    block = (cz, cx, cy)
    at_z, at_x, at_y = iota(block, 0), iota(block, 1), iota(block, 2)
    cuts = [
        at_z == 0,
        at_z == cz - 1,
        jnp.where(at_x == 0, starts, 0) > 0,
        jnp.where(at_x == cx - 1, ends, 0) > 0,
        at_y == 0,
        at_y == cy - 1,
    ]
    coarse_inverse = 1.0 / coarse_diag
    for channel in range(6):
        operator[channel, :, cx : 2 * cx, :] = jnp.where(
            cuts[channel], 0.0, coarse[1 + channel] * coarse_inverse
        )
    operator[6, :, cx : 2 * cx, :] = coarse_inverse

    def operator_copy(channel, side):
        start = 0 if side else 2 * cx
        return remote(
            operator.at[channel, :, cx : 2 * cx, :],
            operator.at[channel, :, start : start + cx, :],
            op_send.at[channel, side], op_recv.at[channel, side], 2 * side - 1, 0,
        )

    row = iota((across, height), 0)
    tile = row + iota((across, height), 1)
    layer_row = iota((depth, height), 0)
    layer_tile = layer_row + iota((depth, height), 1)

    def send_layers(step, turn):
        for side, z in enumerate((0, top)):
            for beside in range(2):
                for layer in range(DEEP - 1):
                    at = beside * (DEEP - 1) + layer
                    layer_stage[step, side, at : at + 1, :] = halo[turn, beside, layer, z : z + 1, :]
        start_z(functools.partial(layer_copy, step))

    def relaxed(z, step, sides):
        v = field[z]
        below = field[z - 1] if z > 0 else z_low[step]
        over = field[z + 1] if z < top else z_high[step]
        out = weights[6, z] + weights[0, z] * below + weights[1, z] * over
        west = jnp.where(row == 0, sides[0][z : z + 1, :], pltpu.roll(v, 1, 0))
        out = out + weights[2, z] * west
        east = jnp.where(row == across - 1, sides[1][z : z + 1, :], pltpu.roll(v, across - 1, 0))
        out = out + weights[3, z] * east
        out = out + weights[4, z] * pltpu.roll(v, 1, 1)
        out = out + weights[5, z] * pltpu.roll(v, height - 1, 1)
        return v, out

    def relax_layer(step, turn, side, layer, inner, outer):
        h = halo[turn, side, layer]
        w = halo_weights.at[side, layer]
        at = side * (DEEP - 1) + layer
        below = jnp.where(layer_row == 0, layer_low[step, at : at + 1, :], pltpu.roll(h, 1, 0))
        over = jnp.where(layer_row == top, layer_high[step, at : at + 1, :], pltpu.roll(h, top, 0))
        west, east = (inner, outer) if side else (outer, inner)
        out = w[6] + w[0] * below + w[1] * over + w[2] * west + w[3] * east
        out = out + w[4] * pltpu.roll(h, 1, 1) + w[5] * pltpu.roll(h, height - 1, 1)
        colour = layer_tile + step + (layer if side else layer + 1)
        halo[turn, side, layer] = jnp.where(colour % 2 == 0, out, h)

    def pack_border(side, layer, z, at):
        border[side, z : z + 1, :] = field[z, at : at + 1, :]

    inner_planes = list(range(1, top))

    def half_sweep(turn, inside):
        step = turn * DEEP + inside
        colours = [(tile + step + z) % 2 == 0 for z in range(2)]

        def update(z):
            v, out = relaxed(z, step, [halo.at[turn, side, 0] for side in range(2)])
            field[z] = jnp.where(colours[z % 2], out, v)

        arrive_z(functools.partial(z_copy, step))
        update(0)
        update(top)
        send_z(step + 1)

        @pl.when(step > 0)
        def _():
            start_x(functools.partial(operator_copy, step - 1))

        for z in inner_planes:
            update(z)
        if inside < DEEP - 1:

            @pl.when(turn == 0)
            def _():
                arrive_x(functools.partial(weight_copy, inside))

            arrive_z(functools.partial(layer_copy, step))
            for layer in range(inside, -1, -1):
                for side in range(2):
                    if layer > 0:
                        inner = halo[turn, side, layer - 1]
                    else:
                        inner = border[side] if inside else x_stage[turn, side, 0]
                    outer = halo[turn, side, layer + 1]
                    relax_layer(step - layer, turn, side, layer, inner, outer)
            if inside + 1 < DEEP - 1:
                send_layers(step + 1, turn)
                pack(pack_border, 1)

    def exchange_x(turn):
        @pl.when(turn > 0)
        def _():
            send_x(turn)

        arrive_x(functools.partial(x_copy, turn))
        send_layers(turn * DEEP, turn)

    def full_round(turn, carry):
        exchange_x(turn)
        for inside in range(DEEP):
            half_sweep(turn, inside)
        return carry

    last = ROUNDS - 1
    lax.fori_loop(0, last, full_round, 0)
    exchange_x(last)
    for inside in range(STEPS - last * DEEP):
        half_sweep(last, inside)
    residual = [None] * depth

    def take_residual(z):
        v, out = relaxed(z, STEPS, [halo.at[last, side, 0] for side in range(2)])
        residual[z] = diag[z] * (out - v)

    for z in inner_planes:
        take_residual(z)
    arrive_z(functools.partial(z_copy, STEPS))
    take_residual(0)
    take_residual(top)
    residual = jnp.stack(residual)

    offset = fine_y - 2 * coarse_y
    restrict = jnp.where(
        (offset == 0) | (offset == 1), 0.75, jnp.where((offset == -1) | (offset == 2), 0.25, 0.0)
    )
    along_y = DOT(residual.reshape(depth * across, height), restrict)
    along_y = along_y.reshape(depth, across, cy)
    edge_stage[0] = 0.25 * along_y[0]
    edge_stage[1] = 0.25 * along_y[depth - 1]
    base = 8
    own = base + across
    for z in range(cz):
        value = 0.75 * along_y[2 * z] + 0.75 * along_y[2 * z + 1]
        if z > 0:
            value = value + 0.25 * along_y[2 * z - 1]
        if z < cz - 1:
            value = value + 0.25 * along_y[2 * z + 2]
        window[z, own : own + across, :] = value
        own_stage[z] = value

    def window_copy(dx, dz, which):
        start = own - across * dx
        rows = slice(start, start + across)
        if dz == 0:
            src, dst = own_stage, window.at[:, rows, :]
        elif dz < 0:
            src, dst = edge_stage.at[0], edge_high.at[rows, :]
        else:
            src, dst = edge_stage.at[1], edge_low.at[rows, :]
        return pltpu.make_async_remote_copy(
            src_ref=src,
            dst_ref=dst,
            send_sem=rhs_send.at[which],
            recv_sem=rhs_recv.at[which],
            device_id=target(dx, dz),
            device_id_type=MESH,
        )

    for which, (dx, dz) in enumerate(around):
        pl.when(exists(dx, dz))(window_copy(dx, dz, which).start)
    for which, (dx, dz) in enumerate(around):
        pl.when(exists(-dx, -dz))(window_copy(dx, dz, which).wait_recv)
    for channel in range(7):
        arrive_x(functools.partial(operator_copy, channel))

    window[0] = window[0] + edge_low[...]
    window[cz - 1] = window[cz - 1] + edge_high[...]
    span = 3 * cx

    def take(offset):
        return window[:, pl.ds(base + offset, span, stride=2), :]

    rhs = 0.25 * take(-1) + 0.75 * take(0) + 0.75 * take(1) + 0.25 * take(2)
    rhs = rhs * operator[6]
    shape = (cz, span, cy)
    coarse_parity = (iota(shape, 0) + iota(shape, 1) + cx + iota(shape, 2)) % 2
    result = jnp.where(coarse_parity == 0, rhs, 0.0)
    for half in range(1, 2 * COARSE_SWEEPS):
        u = result
        out = rhs
        out = out + operator[0] * jnp.concatenate([u[-1:], u[:-1]], axis=0)
        out = out + operator[1] * jnp.concatenate([u[1:], u[:1]], axis=0)
        out = out + operator[2] * pltpu.roll(u, 1, 1)
        out = out + operator[3] * pltpu.roll(u, span - 1, 1)
        out = out + operator[4] * pltpu.roll(u, 1, 2)
        out = out + operator[5] * pltpu.roll(u, cy - 1, 2)
        result = jnp.where(coarse_parity == half % 2, out, u)

    correction = result[:, cx : 2 * cx, :]
    correction_ref[...] = correction
    flat = correction.reshape(cz * cx, cy)
    repeat = jnp.where(iota((cy, height), 0) == iota((cy, height), 1) // 2, 1.0, 0.0)
    wider = DOT(flat, repeat).reshape(cz, cx, height)
    for half in range(height // cy):
        piece = wider[:, :, half * cy : (half + 1) * cy]
        for which in range(2):
            spread[half, :, pl.ds(which, cx, stride=2), :] = piece
    for z in range(depth):
        for half in range(height // cy):
            lanes = slice(half * cy, (half + 1) * cy)
            pressure_ref[z, :, lanes] = field[z, :, lanes] + spread[half, z // 2]

    def drain_z(copy):
        def one(step, carry):
            for side in range(2):
                pl.when(above[2 * side - 1])(copy(step, side).wait_send)
            return carry

        return one

    def drain_x(copy):
        for side in range(2):
            pl.when(there[2 * side - 1])(copy(side).wait_send)

    lax.fori_loop(0, STEPS + 1, drain_z(z_copy), 0)
    for step in range(STEPS):
        if step % DEEP < DEEP - 1:
            drain_z(layer_copy)(step, 0)
    for turn in range(ROUNDS):
        drain_x(functools.partial(x_copy, turn))
    for layer in range(DEEP - 1):
        drain_x(functools.partial(weight_copy, layer))
    for channel in range(7):
        drain_x(functools.partial(operator_copy, channel))
    for which, (dx, dz) in enumerate(around):
        pl.when(exists(dx, dz))(window_copy(dx, dz, which).wait_send)


def body(n_wide, n_narrow, source, start_pressure, reaction, couplings, run_lengths):
    depth, across, height = source.shape
    cz, cx, cy = depth // 2, across // 2, height // 2
    f32 = jnp.float32
    fine = (depth, across, height)
    steps = STEPS + 1
    layers = DEEP - 1
    face = 2 * layers
    dma = pltpu.SemaphoreType.DMA
    hbm = pl.BlockSpec(memory_space=pltpu.HBM)
    vmem = pl.BlockSpec(memory_space=pltpu.VMEM)
    return pl.pallas_call(
        functools.partial(kernel, n_wide, n_narrow),
        out_shape=(
            jax.ShapeDtypeStruct(fine, f32),
            jax.ShapeDtypeStruct((cz, cx, cy), f32),
        ),
        in_specs=[pl.BlockSpec(memory_space=pltpu.SMEM)] + [hbm] * 4,
        out_specs=(vmem, vmem),
        scratch_shapes=[
            pltpu.VMEM(fine, f32),
            pltpu.VMEM(fine, f32),
            pltpu.VMEM((6,) + fine, f32),
            pltpu.VMEM(fine, f32),
            pltpu.VMEM((7,) + fine, f32),
            pltpu.VMEM(fine, f32),
            pltpu.VMEM((ROUNDS, 2, DEEP, depth, height), f32),
            pltpu.VMEM((ROUNDS, 2, DEEP, depth, height), f32),
            pltpu.VMEM((2, depth, height), f32),
            pltpu.VMEM((2, layers, 7, depth, height), f32),
            pltpu.VMEM((2, layers, 7, depth, height), f32),
            pltpu.VMEM((steps, across, height), f32),
            pltpu.VMEM((steps, across, height), f32),
            pltpu.VMEM((steps, 2, across, height), f32),
            pltpu.VMEM((steps, face, height), f32),
            pltpu.VMEM((steps, face, height), f32),
            pltpu.VMEM((steps, 2, face, height), f32),
            pltpu.VMEM((7, cz, across, cy), f32),
            pltpu.VMEM((7, cz, 3 * cx, cy), f32),
            pltpu.VMEM((cz, 3 * across + 16, cy), f32),
            pltpu.VMEM((3 * across + 16, cy), f32),
            pltpu.VMEM((3 * across + 16, cy), f32),
            pltpu.VMEM((2, across, cy), f32),
            pltpu.VMEM((cz, across, cy), f32),
            pltpu.VMEM((2, cz, across, cy), f32),
            dma((4,)),
            dma((ROUNDS, 2)),
            dma((ROUNDS, 2)),
            dma((steps, 2)),
            dma((steps, 2)),
            dma((steps, 2)),
            dma((steps, 2)),
            dma((layers, 2)),
            dma((layers, 2)),
            dma((7, 2)),
            dma((7, 2)),
            dma((8,)),
            dma((8,)),
        ],
        compiler_params=pltpu.CompilerParams(
            collective_id=0, has_side_effects=True, vmem_limit_bytes=32 * 1024 * 1024
        ),
    )(run_lengths, source, start_pressure, reaction, couplings)


def solution(mesh):
    placed = (
        P("narrow", "wide", None),
        P("narrow", "wide", None),
        P("narrow", "wide", None),
        P(None, "narrow", "wide", None),
        P(),
    )
    return jax.shard_map(
        functools.partial(body, mesh.shape["wide"], mesh.shape["narrow"]),
        mesh=mesh,
        in_specs=placed,
        out_specs=(P("narrow", "wide", None), P("narrow", "wide", None)),
        check_vma=False,
    )
```
